128 devices in a mesh: branch: 2 (over x_lo), seq: 16 (over x_hi, z, core), tp: 4 (over y).
Axes of the slice: x: 4 (x_hi: 2, x_lo: 2; x = x_hi * 2 + x_lo), y: 4, z: 4, core: 2. Of those that a mesh axis runs over, the one named last changes fastest.
Arguments:
- hidden: bfloat16 [2, 8192, 4096], P('branch', 'seq', 'tp'), may hold values from -6 to 6
- modulation: float32 [2, 4, 4096], P('branch'), may hold values from -4 to 4
- qkv_weight: bfloat16 [2, 4096, 3, 2048], P('branch', None, None, 'tp'), as said below
- out_weight: bfloat16 [2, 2048, 4096], P('branch', 'tp'), may hold values from -0.5 to 0.5
- control_proj: bfloat16 [4096, 4096], P('tp'), may hold values from -0.09375 to 0.09375
- cached_mlp: bfloat16 [2, 8192, 4096], P('branch', 'seq', 'tp'), may hold values from -6 to 6
Outputs:
- updated: bfloat16 [2, 8192, 4096], P('branch', 'seq', 'tp')
The draws below stay inside these ranges and needn't reach their ends.
Inputs may be any that keep to these rules, and one draw needn't show every extreme that they name: `qkv_weight`: entries are of order 4096^-1/2 times a factor.
All inputs are finite; a program needn't handle non-finite values.
Results may differ from the reference program's by a relative error of at most 0.02.
Values may be sent and summed in bfloat16 or wider, within the bound.
No kernel may reach another device: no remote copies, remote signals or barrier semaphores. Data moves between devices by JAX's collectives and lax.ppermute only.
A program may use at most 256 MiB of HBM per device.

```python
import jax
import jax.numpy as jnp
from jax import lax

D = 4096
HEAD_DIM = 128
HEADS = 16
TOKENS = 8192
QW = 2048


def draw_qkv_weight(key, part):
    key = jax.random.fold_in(key, 11)
    first = jax.random.fold_in(key, 0)
    base = jax.random.truncated_normal(first, -4.0, 4.0, (2, D, 3, QW), jnp.float32) * D ** (-0.5)
    factors = jnp.array([1.5, 1.5, 1.0], jnp.float32).reshape(1, 1, 3, 1)
    base = base * factors
    return base.astype(jnp.bfloat16)


def block_scale(own_key, extent, cuts, smallest, top_value):
    level = 1.0
    for dim, shards_of in cuts:
        draws = jax.random.uniform(jax.random.fold_in(jax.random.fold_in(own_key, 6), dim), (shards_of,), jnp.float32, smallest / len(cuts), top_value / len(cuts))
        level = level * jnp.repeat(jnp.exp(draws), extent[dim] // shards_of).reshape((-1,) + (1,) * (len(extent) - 1 - dim))
    return level


def scatter_about(key, extent, scale, bound, pieces=(), held_as=jnp.bfloat16):
    loudness = block_scale(key, extent, pieces, -0.22, 0.18) if pieces else 1.0
    drawn = jax.random.normal(key, extent, jnp.float32) * scale * loudness
    return jnp.minimum(jnp.maximum(drawn, -bound), bound).astype(held_as)


def setup_inputs(seed: int = 0) -> dict:
    keys = jax.random.split(jax.random.key(seed), 7)
    hidden = scatter_about(keys[0], (2, TOKENS, D), 1.0, 6.0, ((0, 2), (1, 16), (2, 4)))
    modulation = scatter_about(keys[1], (2, 4, D), 0.7, 4.0, ((0, 2),), jnp.float32)
    qkv_weight = draw_qkv_weight(jax.random.fold_in(keys[6], 71), 0)
    out_weight = scatter_about(keys[3], (2, QW, D), (QW // 16) ** -0.5, 0.5, ((0, 2), (1, 4)))
    control_proj = scatter_about(keys[4], (D, D), D ** -0.5, 0.09375, ((0, 4),))
    cached_mlp = scatter_about(keys[5], (2, TOKENS, D), 1.0, 6.0, ((0, 2), (1, 16), (2, 4)))
    return dict(hidden=hidden, modulation=modulation, qkv_weight=qkv_weight, out_weight=out_weight, control_proj=control_proj, cached_mlp=cached_mlp)


def run_block(tokens_in, modulation_rows, qkv_rows, out_rows, cache_rows):
    widened = tokens_in.astype(jnp.float32)
    row_mean = lax.optimization_barrier(jnp.mean(widened, axis=-1, keepdims=True))
    centred = widened - row_mean
    row_var = lax.optimization_barrier(jnp.mean(centred * centred, axis=-1, keepdims=True))
    normed = centred * lax.rsqrt(row_var + 1e-06)
    modulated = (normed * (1.0 + modulation_rows[1]) + modulation_rows[0]).astype(jnp.bfloat16)
    projected = jnp.einsum('td,dcw->ctw', modulated.astype(jnp.float32), qkv_rows.astype(jnp.float32))
    projected = projected.astype(jnp.bfloat16)
    row_total = projected.shape[1]
    query = projected[0].reshape(row_total, HEADS, HEAD_DIM).transpose(1, 0, 2)
    key_rows = projected[1].reshape(row_total, HEADS, HEAD_DIM).transpose(1, 0, 2)
    value_rows = projected[2].reshape(row_total, HEADS, HEAD_DIM).transpose(1, 0, 2)
    score_scale = 1.0 / HEAD_DIM ** 0.5

    def one_head(triple):
        head_query, head_keys, head_values = triple
        scores = jnp.dot(head_query, head_keys.T, preferred_element_type=jnp.float32) * score_scale
        weights = jax.nn.softmax(scores, axis=-1).astype(jnp.bfloat16)
        return jnp.dot(weights, head_values, preferred_element_type=jnp.float32)
    attended = lax.map(one_head, (query, key_rows, value_rows))
    attended = attended.transpose(1, 0, 2).reshape(row_total, HEADS * HEAD_DIM).astype(jnp.bfloat16)
    attention = jnp.dot(attended, out_rows, preferred_element_type=jnp.float32)
    return widened + modulation_rows[2] * attention + modulation_rows[3] * cache_rows.astype(jnp.float32)

def reference(hidden, modulation, qkv_weight, out_weight, control_proj, cached_mlp):
    control_blend = run_block(hidden[0], modulation[0], qkv_weight[0], out_weight[0], cached_mlp[0])
    control_out = control_blend.astype(jnp.bfloat16)
    residual = jnp.dot(control_out, control_proj, preferred_element_type=jnp.float32)
    main_blend = run_block(hidden[1], modulation[1], qkv_weight[1], out_weight[1], cached_mlp[1])
    main_out = (main_blend + residual).astype(jnp.bfloat16)
    return jnp.stack([control_out, main_out])
```

```python
import functools

import jax
import jax.numpy as jnp
from jax import lax
from jax.experimental import pallas as pl
from jax.experimental.pallas import tpu as pltpu
from jax.sharding import PartitionSpec as P

HEAD_DIM = 128
ROWS = 512
WIDE = 1024
COLS = 512
HEADS_HERE = 4
Q_SCALE = 1.4426950408889634 / HEAD_DIM**0.5
NT = (((1,), (1,)), ((), ()))
VMEM_LIMIT = 58 * 2**20


def cost(flops):
    return pl.CostEstimate(flops=int(flops), bytes_accessed=2**20, transcendentals=0)


def seq_pairs(move):
    where = [(h, z, c) for h in range(2) for z in range(4) for c in range(2)]
    index = lambda h, z, c: h * 8 + z * 2 + c
    return [(index(*p), index(*move(*p))) for p in where]


def along_z(value, by):
    return lax.ppermute(value, "seq", seq_pairs(lambda h, z, c: (h, (z + by) % 4, c)))


def across_x(value):
    return lax.ppermute(value, "seq", seq_pairs(lambda h, z, c: (1 - h, z, c)))


def across_cores(value):
    return lax.ppermute(value, "seq", seq_pairs(lambda h, z, c: (h, z, 1 - c)))


def along_y(value, by):
    return lax.ppermute(value, "tp", [(i, (i + by) % 4) for i in range(4)])


def after(value, *others):
    return lax.optimization_barrier((value, others))[0]


def gathered_y(value):
    one, three = along_y(value, 1), along_y(value, 3)
    return [one, along_y(value, 2), three]


def qkv_kernel(place, tokens, mod, weight, *rest):
    out, modulated, held, arrived, whole, landed = rest[-6:]
    z = place[1]
    rows = modulated.shape[0]
    quarter = rows // 4
    tile = 16
    lands = []
    for part in range(4):
        here = pl.ds(part * quarter, quarter)
        lands.append(pltpu.make_async_copy(tokens.at[here], whole.at[here], landed.at[part]))
    copies = []
    for c in range(3):
        for k in range(4):
            here = pl.ds(k * WIDE, WIDE)
            copies.append(
                pltpu.make_async_copy(weight.at[c, here], held.at[c, here], arrived.at[c * 4 + k])
            )
    for copy in lands + copies:
        copy.start()

    for first in range(0, rows, tile):
        if first % quarter == 0:
            lands[first // quarter].wait()
        here = pl.ds(first, tile)
        total = 0.0
        for k in range(4):
            part = whole[here, k * WIDE : (k + 1) * WIDE].astype(jnp.float32)
            total = total + jnp.sum(part, axis=1, keepdims=True)
        mean = total * (1.0 / (4 * WIDE))
        square = 0.0
        for k in range(4):
            part = whole[here, k * WIDE : (k + 1) * WIDE].astype(jnp.float32) - mean
            square = square + jnp.sum(part * part, axis=1, keepdims=True)
        scale = lax.rsqrt(square * (1.0 / (4 * WIDE)) + 1e-06)
        for k in range(4):
            columns = pl.ds(k * WIDE, WIDE)
            part = (whole[here, columns].astype(jnp.float32) - mean) * scale
            value = part * (1.0 + mod[1:2, columns]) + mod[0:1, columns]
            modulated[here, columns] = value.astype(jnp.bfloat16)

    for c in range(3):
        for copy in copies[c * 4 : c * 4 + 4]:
            copy.wait()
        product = jnp.dot(modulated[...], held[c], preferred_element_type=jnp.float32)
        if c == 0:
            product = product * Q_SCALE
        product = product.astype(jnp.bfloat16)
        for head in range(HEADS_HERE):
            slot = lax.rem(head + 4 - z, 4)
            out[slot, c] = product[:, head * HEAD_DIM : (head + 1) * HEAD_DIM]


def qkv(place, tokens, mod, weight, earlier):
    rows = tokens.shape[0]
    hbm = pl.BlockSpec(memory_space=pl.ANY)
    vmem = pl.BlockSpec(memory_space=pltpu.VMEM)
    return pl.pallas_call(
        qkv_kernel,
        in_specs=[pl.BlockSpec(memory_space=pltpu.SMEM), hbm, vmem, hbm] + [hbm] * len(earlier),
        out_specs=vmem,
        scratch_shapes=[
            pltpu.VMEM((rows, 4 * WIDE), jnp.bfloat16),
            pltpu.VMEM((3, 4 * WIDE, COLS), jnp.bfloat16),
            pltpu.SemaphoreType.DMA((12,)),
            pltpu.VMEM((rows, 4 * WIDE), jnp.bfloat16),
            pltpu.SemaphoreType.DMA((4,)),
        ],
        out_shape=jax.ShapeDtypeStruct((4, 3, rows, HEAD_DIM), jnp.bfloat16),
        compiler_params=pltpu.CompilerParams(vmem_limit_bytes=VMEM_LIMIT),
        cost_estimate=cost(2 * rows * 4 * WIDE * 3 * COLS),
        name="qkv",
    )(place, tokens, mod, weight, *earlier)


def attention_kernel(*refs, count, gates, first, last):
    query = refs[0][...]
    pairs = refs[1 : 1 + count]
    rest = refs[1 + count + gates :]
    rows = query.shape[0]
    step = 1024
    pieces = [(pair, at) for pair in pairs for at in range(0, pair.shape[1], step)]

    def scores_of(piece):
        pair, at = piece
        keys = pair[0, pl.ds(at, step), :]
        return lax.dot_general(query, keys, NT, preferred_element_type=jnp.float32)

    if first:
        top = jnp.full((rows, 1), -1e30, jnp.float32)
        total = jnp.zeros((rows, 1), jnp.float32)
        weighted = jnp.zeros((rows, HEAD_DIM), jnp.float32)
    else:
        weighted = rest[0][...]
        top = jnp.max(rest[1][...], axis=1, keepdims=True)
        total = jnp.max(rest[2][...], axis=1, keepdims=True)
        rest = rest[3:]
    ready = scores_of(pieces[0])
    for index, (pair, at) in enumerate(pieces):
        scores = ready
        if index + 1 < len(pieces):
            ready = scores_of(pieces[index + 1])
        new_top = jnp.maximum(top, jnp.max(scores, axis=1, keepdims=True))
        weights = jnp.exp2(scores - new_top)
        fade = jnp.exp2(top - new_top)
        total = total * fade + jnp.sum(weights, axis=1, keepdims=True)
        values = pair[1, pl.ds(at, step), :]
        update = jnp.dot(weights.astype(jnp.bfloat16), values, preferred_element_type=jnp.float32)
        weighted = weighted * fade + update
        top = new_top
    if last:
        rest[0][...] = (weighted / total).astype(jnp.bfloat16)
    else:
        rest[0][...] = weighted
        rest[1][...] = jnp.broadcast_to(top, (rows, HEAD_DIM))
        rest[2][...] = jnp.broadcast_to(total, (rows, HEAD_DIM))


def attention(query, pairs, carry, last, part, parts, earlier=()):
    rows = query.shape[0] // parts
    block = 512
    first = part * (rows // block)
    tokens = sum(pair.shape[1] for pair in pairs)
    row_block = pl.BlockSpec((block, HEAD_DIM), lambda i: (i, 0))
    in_block = pl.BlockSpec((block, HEAD_DIM), lambda i: (first + i, 0))
    shape = lambda dtype: jax.ShapeDtypeStruct((rows, HEAD_DIM), dtype)
    if last:
        out_shape, out_specs = shape(jnp.bfloat16), row_block
    else:
        out_shape, out_specs = [shape(jnp.float32)] * 3, [row_block] * 3
    return pl.pallas_call(
        functools.partial(attention_kernel, count=len(pairs), gates=len(earlier), first=not carry, last=last),
        grid=(rows // block,),
        in_specs=[in_block]
        + [pl.BlockSpec(pair.shape, lambda i: (0, 0, 0)) for pair in pairs]
        + [pl.BlockSpec(memory_space=pl.ANY)] * len(earlier)
        + [in_block] * len(carry),
        out_specs=out_specs,
        out_shape=out_shape,
        compiler_params=pltpu.CompilerParams(vmem_limit_bytes=VMEM_LIMIT),
        cost_estimate=pl.CostEstimate(
            flops=4 * rows * tokens * HEAD_DIM,
            bytes_accessed=4 * tokens * HEAD_DIM,
            transcendentals=rows * tokens,
        ),
        name="attention",
    )(query, *pairs, *earlier, *carry)


def output_kernel(place, *refs, addends, first, count):
    blocks, weights, scale, terms = refs[:4], refs[4 : 4 + count], refs[4 + count], refs[5 + count : -3]
    out, held, arrived = refs[-3:]
    y, z, branch, core, x_hi = place[0], place[1], place[2], place[3], place[4]
    rows = out.shape[0]
    copies = []
    for index in range(4):
        to = held.at[pl.ds(index * 4, 4)]
        source = weights[0].at[pl.ds(index * 4, 4)] if count == 1 else weights[index]
        copies.append(pltpu.make_async_copy(source, to, arrived.at[index]))
        copies[-1].start()

    def rows_of(back, by):
        row, head = lax.rem(y + 4 - back, 4), lax.rem(z + by, 4)
        if count == 1:
            return held[pl.ds(head * 4, 4), row].reshape(HEAD_DIM, WIDE)
        parts = []
        for i in range(4):
            across = lax.rem(head // 2 + x_hi, 2)
            behind = lax.rem(z + 4 - lax.rem(head, 2) * 2 - i // 2, 4)
            parts.append(held[lax.rem(i % 2 + core, 2) * 8 + across * 4 + behind, row])
        return jnp.concatenate(parts, axis=0)

    product = None
    for copy in copies:
        copy.wait()
    for back in range(4):
        share = jnp.concatenate([rows_of(back, by) for by in range(4)], axis=0)
        left = jnp.concatenate([blocks[back][by, pl.ds(first, rows), :] for by in range(4)], axis=1)
        update = jnp.dot(left, share, preferred_element_type=jnp.float32)
        product = update if product is None else product + update
    if addends == "early":
        out[...] = (product + terms[0][...].astype(jnp.float32)).astype(out.dtype)
    elif addends == "none":
        out[...] = product.astype(out.dtype)
    else:
        value = terms[0][...].astype(jnp.float32) + scale[0:1, :] * product
        out[...] = value + scale[1:2, :] * terms[1][...].astype(jnp.float32)
        half = terms[2].shape[0]
        early = terms[2][...].astype(jnp.float32)
        out[pl.ds(half, half), :] += branch.astype(jnp.float32) * early


def output(place, blocks, weights, scale, terms, addends, first, rows, dtype, name):
    vmem = pl.BlockSpec(memory_space=pltpu.VMEM)
    return pl.pallas_call(
        functools.partial(
            output_kernel, addends=addends, first=first, count=len(weights)
        ),
        in_specs=[pl.BlockSpec(memory_space=pltpu.SMEM)]
        + [vmem] * len(blocks)
        + [pl.BlockSpec(memory_space=pl.ANY)] * len(weights)
        + [vmem] * (1 + len(terms)),
        out_specs=vmem,
        scratch_shapes=[
            pltpu.VMEM((16, 4, 32, WIDE), jnp.bfloat16),
            pltpu.SemaphoreType.DMA((4,)),
        ],
        out_shape=jax.ShapeDtypeStruct((rows, WIDE), dtype),
        compiler_params=pltpu.CompilerParams(vmem_limit_bytes=VMEM_LIMIT),
        cost_estimate=cost(2 * rows * 2048 * WIDE),
        name=name,
    )(place, *blocks, *weights, scale, *terms)


def body(hidden, modulation, qkv_weight, out_weight, control_proj, cached_mlp):
    hidden, cached = hidden[0], cached_mlp[0]
    mod = modulation[0]
    branch = lax.axis_index("branch")
    y = lax.axis_index("tp")
    s = lax.axis_index("seq")
    z = lax.rem(s // 2, 4)
    place = jnp.stack([y, z, branch, lax.rem(s, 2), s // 8]).astype(jnp.int32)
    gates = lax.dynamic_slice_in_dim(mod[2:4], y * WIDE, WIDE, 1)
    turn = lambda by: lax.rem(y + by, 4)
    rows = ROWS // 2
    weight = qkv_weight[0].transpose(1, 0, 2)

    def sent_y(value):
        cut = lambda by: lax.dynamic_slice_in_dim(value, turn(by) * WIDE, WIDE, 1)
        return [cut(0)] + [along_y(cut(by), by) for by in (1, 2, 3)]

    def heads_turned(part):
        return [part[0]] + [along_z(part[by], by) for by in (1, 2, 3)]

    tokens = lax.all_gather(hidden, "tp", axis=1, tiled=True)

    with jax.named_scope("early_residual"):
        base = (hidden.astype(jnp.float32) + gates[1] * cached.astype(jnp.float32)).astype(jnp.bfloat16)
        sent = lax.ppermute(base[rows:], "branch", [(0, 1)])
        base = jnp.where(branch == 0, base[:rows], sent)

    with jax.named_scope("out_weight_columns"):
        share = lax.dynamic_slice_in_dim(out_weight[0], s * 32, 32, 0)
        turned = jnp.stack(sent_y(share))
        ordered = jnp.stack(
            [lax.dynamic_index_in_dim(turned, turn(4 - row), 0, keepdims=False) for row in range(4)]
        )
        of_z = jnp.stack([ordered] + [along_z(ordered, by) for by in (1, 2, 3)])

    with jax.named_scope("early_residual"):
        early = jnp.dot(base, control_proj, preferred_element_type=jnp.float32).astype(jnp.bfloat16)

    with jax.named_scope("joint_weight"):
        gated = (ordered.reshape(128, WIDE).astype(jnp.float32) * gates[0]).astype(jnp.bfloat16)
        joint = jnp.dot(gated, control_proj, preferred_element_type=jnp.float32).astype(jnp.bfloat16)

    with jax.named_scope("out_weight_columns"):
        of_x = across_x(after(of_z, sent))

    with jax.named_scope("joint_weight"):
        joint_share = lax.psum_scatter(joint, "tp", scatter_dimension=1, tiled=True)
    projected = qkv(place, tokens, mod, weight, [early, joint, of_x])
    with jax.named_scope("early_residual"):
        early = lax.psum_scatter(after(early, projected), "tp", scatter_dimension=1, tiled=True)

    turned = heads_turned(projected)
    with jax.named_scope("out_weight_columns"):
        mine = after([of_z, of_x], projected)
        out_columns = mine + [across_cores(part) for part in mine]
    query = jnp.concatenate([block[0] for block in turned], axis=0)
    near = jnp.concatenate([block[1:3] for block in turned], axis=1)
    far = across_x(near)
    carry = attention(query, [near, across_cores(near)], [], False, 0, 1, out_columns)
    far = after(far, carry)
    with jax.named_scope("joint_weight"):
        joint_share = after(joint_share, far, early).reshape(4, 32, WIDE)
        joint_columns = lax.all_gather(joint_share, "seq", axis=0)
    attended = attention(query, [far, across_cores(far)], carry, True, 0, 1)

    attended = attended.reshape(4, ROWS, HEAD_DIM)
    attended = jnp.stack([attended[0]] + [along_z(attended[by], 4 - by) for by in (1, 2, 3)])
    group = [attended, *gathered_y(attended)]
    joined = []
    for half in range(2):
        terms, kind = ([early], "early") if half == 0 else ([], "none")
        residual = output(
            place, group, [joint_columns], gates, terms, kind, half * rows, rows, jnp.bfloat16, "residual"
        )
        joined.append(lax.ppermute(residual, "branch", [(0, 1)]))
    terms = [hidden, cached, early]
    blended = output(
        place, group, out_columns, gates, terms, "blended", 0, ROWS, jnp.float32, "blended"
    )
    joined = jnp.concatenate(joined, axis=0)
    return (blended + joined.astype(jnp.float32)).astype(jnp.bfloat16)[None]


def solution(mesh):
    placed = (
        P("branch", "seq", "tp"),
        P("branch", None, None),
        P("branch", None, None, "tp"),
        P("branch", "tp", None),
        P("tp", None),
        P("branch", "seq", "tp"),
    )
    return jax.shard_map(
        body, mesh=mesh, in_specs=placed, out_specs=P("branch", "seq", "tp"), check_vma=False
    )
```

```python
import functools

import jax
import jax.numpy as jnp
from jax import lax
from jax.experimental import pallas as pl
from jax.experimental.pallas import tpu as pltpu
from jax.sharding import PartitionSpec as P

HEAD_DIM = 128
ROWS = 512
WIDE = 1024
COLS = 512
HEADS_HERE = 4
Q_SCALE = 1.4426950408889634 / HEAD_DIM**0.5
NT = (((1,), (1,)), ((), ()))
VMEM_LIMIT = 58 * 2**20


def cost(flops):
    return pl.CostEstimate(flops=int(flops), bytes_accessed=2**20, transcendentals=0)


def seq_pairs(move):
    where = [(h, z, c) for h in range(2) for z in range(4) for c in range(2)]
    index = lambda h, z, c: h * 8 + z * 2 + c
    return [(index(*p), index(*move(*p))) for p in where]


def along_z(value, by):
    return lax.ppermute(value, "seq", seq_pairs(lambda h, z, c: (h, (z + by) % 4, c)))


def across_x(value):
    return lax.ppermute(value, "seq", seq_pairs(lambda h, z, c: (1 - h, z, c)))


def across_cores(value):
    return lax.ppermute(value, "seq", seq_pairs(lambda h, z, c: (h, z, 1 - c)))


def along_y(value, by):
    return lax.ppermute(value, "tp", [(i, (i + by) % 4) for i in range(4)])


def after(value, *others):
    return lax.optimization_barrier((value, others))[0]


def gathered_y(value):
    one, three = along_y(value, 1), along_y(value, 3)
    return [one, along_y(value, 2), three]


def qkv_kernel(place, tokens, mod, weight, *rest):
    out, modulated, held, arrived, whole, landed = rest[-6:]
    z = place[1]
    rows = modulated.shape[0]
    quarter = rows // 4
    tile = 16
    lands = []
    for part in range(4):
        here = pl.ds(part * quarter, quarter)
        lands.append(pltpu.make_async_copy(tokens.at[here], whole.at[here], landed.at[part]))
    copies = []
    for c in range(3):
        for k in range(4):
            here = pl.ds(k * WIDE, WIDE)
            copies.append(
                pltpu.make_async_copy(weight.at[c, here], held.at[c, here], arrived.at[c * 4 + k])
            )
    for copy in lands + copies[:4]:
        copy.start()

    for first in range(0, rows, tile):
        if first % quarter == 0:
            lands[first // quarter].wait()
            if first // quarter in (1, 2):
                for copy in copies[first // quarter * 4 : first // quarter * 4 + 4]:
                    copy.start()
        here = pl.ds(first, tile)
        total = 0.0
        for k in range(4):
            part = whole[here, k * WIDE : (k + 1) * WIDE].astype(jnp.float32)
            total = total + jnp.sum(part, axis=1, keepdims=True)
        mean = total * (1.0 / (4 * WIDE))
        square = 0.0
        for k in range(4):
            part = whole[here, k * WIDE : (k + 1) * WIDE].astype(jnp.float32) - mean
            square = square + jnp.sum(part * part, axis=1, keepdims=True)
        scale = lax.rsqrt(square * (1.0 / (4 * WIDE)) + 1e-06)
        for k in range(4):
            columns = pl.ds(k * WIDE, WIDE)
            part = (whole[here, columns].astype(jnp.float32) - mean) * scale
            value = part * (1.0 + mod[1:2, columns]) + mod[0:1, columns]
            modulated[here, columns] = value.astype(jnp.bfloat16)

    for c in range(3):
        for copy in copies[c * 4 : c * 4 + 4]:
            copy.wait()
        product = jnp.dot(modulated[...], held[c], preferred_element_type=jnp.float32)
        if c == 0:
            product = product * Q_SCALE
        product = product.astype(jnp.bfloat16)
        for head in range(HEADS_HERE):
            slot = lax.rem(head + 4 - z, 4)
            out[slot, c] = product[:, head * HEAD_DIM : (head + 1) * HEAD_DIM]


def qkv(place, tokens, mod, weight, earlier):
    rows = tokens.shape[0]
    hbm = pl.BlockSpec(memory_space=pl.ANY)
    vmem = pl.BlockSpec(memory_space=pltpu.VMEM)
    return pl.pallas_call(
        qkv_kernel,
        in_specs=[pl.BlockSpec(memory_space=pltpu.SMEM), hbm, vmem, hbm] + [hbm] * len(earlier),
        out_specs=vmem,
        scratch_shapes=[
            pltpu.VMEM((rows, 4 * WIDE), jnp.bfloat16),
            pltpu.VMEM((3, 4 * WIDE, COLS), jnp.bfloat16),
            pltpu.SemaphoreType.DMA((12,)),
            pltpu.VMEM((rows, 4 * WIDE), jnp.bfloat16),
            pltpu.SemaphoreType.DMA((4,)),
        ],
        out_shape=jax.ShapeDtypeStruct((4, 3, rows, HEAD_DIM), jnp.bfloat16),
        compiler_params=pltpu.CompilerParams(vmem_limit_bytes=VMEM_LIMIT),
        cost_estimate=cost(2 * rows * 4 * WIDE * 3 * COLS),
        name="qkv",
    )(place, tokens, mod, weight, *earlier)


def products_kernel(one, two, right, out_one, out_two):
    for left, out in ((one, out_one), (two, out_two)):
        out[...] = jnp.dot(left[...], right[...], preferred_element_type=jnp.float32).astype(out.dtype)


def products(one, two, right):
    depth, columns = right.shape
    rows = (one.shape[0], two.shape[0])
    return pl.pallas_call(
        products_kernel,
        grid=(columns // WIDE,),
        in_specs=[pl.BlockSpec((count, depth), lambda n: (0, 0)) for count in rows]
        + [pl.BlockSpec((depth, WIDE), lambda n: (0, n))],
        out_specs=[pl.BlockSpec((count, WIDE), lambda n: (0, n)) for count in rows],
        out_shape=[jax.ShapeDtypeStruct((count, columns), jnp.bfloat16) for count in rows],
        compiler_params=pltpu.CompilerParams(vmem_limit_bytes=VMEM_LIMIT),
        cost_estimate=cost(2 * sum(rows) * depth * columns),
        name="products",
    )(one, two, right)


def attention_kernel(*refs, count, gates, first, last):
    query = refs[0][...]
    pairs = refs[1 : 1 + count]
    rest = refs[1 + count + gates :]
    rows = query.shape[0]
    pieces = []
    for pair in pairs:
        step = pair.shape[1] // pl.cdiv(pair.shape[1], 1024)
        pieces += [(pair, pl.ds(at, step)) for at in range(0, pair.shape[1], step)]

    def scores_of(piece):
        pair, at = piece
        keys = pair[0, at, :]
        return lax.dot_general(query, keys, NT, preferred_element_type=jnp.float32)

    if first:
        top = jnp.full((rows, 1), -1e30, jnp.float32)
        total = jnp.zeros((rows, 1), jnp.float32)
        weighted = jnp.zeros((rows, HEAD_DIM), jnp.float32)
    else:
        weighted = rest[0][...]
        top = jnp.max(rest[1][...], axis=1, keepdims=True)
        total = jnp.max(rest[2][...], axis=1, keepdims=True)
        rest = rest[3:]
    ready = scores_of(pieces[0])
    for index, (pair, at) in enumerate(pieces):
        scores = ready
        if index + 1 < len(pieces):
            ready = scores_of(pieces[index + 1])
        new_top = jnp.maximum(top, jnp.max(scores, axis=1, keepdims=True))
        weights = jnp.exp2(scores - new_top)
        fade = jnp.exp2(top - new_top)
        total = total * fade + jnp.sum(weights, axis=1, keepdims=True)
        values = pair[1, at, :]
        update = jnp.dot(weights.astype(jnp.bfloat16), values, preferred_element_type=jnp.float32)
        weighted = weighted * fade + update
        top = new_top
    if last:
        rest[0][...] = (weighted / total).astype(jnp.bfloat16)
    else:
        rest[0][...] = weighted
        rest[1][...] = jnp.broadcast_to(top, (rows, HEAD_DIM))
        rest[2][...] = jnp.broadcast_to(total, (rows, HEAD_DIM))


def attention(query, pairs, carry, last, part, parts, earlier=()):
    rows = query.shape[0] // parts
    block = 512
    first = part * (rows // block)
    tokens = sum(pair.shape[1] for pair in pairs)
    row_block = pl.BlockSpec((block, HEAD_DIM), lambda i: (i, 0))
    in_block = pl.BlockSpec((block, HEAD_DIM), lambda i: (first + i, 0))
    shape = lambda dtype: jax.ShapeDtypeStruct((rows, HEAD_DIM), dtype)
    if last:
        out_shape, out_specs = shape(jnp.bfloat16), row_block
    else:
        out_shape, out_specs = [shape(jnp.float32)] * 3, [row_block] * 3
    return pl.pallas_call(
        functools.partial(attention_kernel, count=len(pairs), gates=len(earlier), first=not carry, last=last),
        grid=(rows // block,),
        in_specs=[in_block]
        + [pl.BlockSpec(pair.shape, lambda i: (0, 0, 0)) for pair in pairs]
        + [pl.BlockSpec(memory_space=pl.ANY)] * len(earlier)
        + [in_block] * len(carry),
        out_specs=out_specs,
        out_shape=out_shape,
        compiler_params=pltpu.CompilerParams(vmem_limit_bytes=VMEM_LIMIT),
        cost_estimate=pl.CostEstimate(
            flops=4 * rows * tokens * HEAD_DIM,
            bytes_accessed=4 * tokens * HEAD_DIM,
            transcendentals=rows * tokens,
        ),
        name="attention",
    )(query, *pairs, *earlier, *carry)


def output_kernel(place, *refs, groups, count):
    blocks, refs = refs[: 4 * groups], refs[4 * groups :]
    weights, scale, terms = refs[:count], refs[count], refs[count + 1 : -3]
    out, held, arrived = refs[-3:]
    y, z, branch, core, x_hi = place[0], place[1], place[2], place[3], place[4]
    rows = out.shape[0]
    copies = []
    for index in range(4):
        to = held.at[pl.ds(index * 4, 4)]
        per = 4 // count
        source = weights[index // per].at[pl.ds(index % per * 4, 4)]
        copies.append(pltpu.make_async_copy(source, to, arrived.at[index]))
        copies[-1].start()

    def rows_of(back, by):
        row, head = lax.rem(y + 4 - back, 4), lax.rem(z + by, 4)
        if count == 1:
            return held[pl.ds(head * 4, 4), row].reshape(HEAD_DIM, WIDE)
        parts = []
        for i in range(4):
            across = lax.rem(head // 2 + x_hi, 2)
            behind = lax.rem(z + 4 - lax.rem(head, 2) * 2 - i // 2, 4)
            parts.append(held[lax.rem(i % 2 + core, 2) * 8 + behind * 2 + across, row])
        return jnp.concatenate(parts, axis=0)

    for copy in copies:
        copy.wait()
    products = [None] * groups
    for back in range(4):
        share = jnp.concatenate([rows_of(back, by) for by in range(4)], axis=0)
        for group in range(groups):
            block = blocks[4 * group + back]
            left = jnp.concatenate([block[by] for by in range(4)], axis=1)
            update = jnp.dot(left, share, preferred_element_type=jnp.float32)
            products[group] = update if back == 0 else products[group] + update
    if count == 1:
        product = products[0]
        if terms:
            product = product + terms[0][...].astype(jnp.float32)
        out[...] = product.astype(out.dtype)
    else:
        for group in range(groups):
            here = pl.ds(group * (rows // groups), rows // groups)
            value = terms[0][here, :].astype(jnp.float32) + scale[0:1, :] * products[group]
            value = value + scale[1:2, :] * terms[1][here, :].astype(jnp.float32)
            if group == 1:
                value = value + branch.astype(jnp.float32) * terms[2][...].astype(jnp.float32)
            out[here, :] = value


def output(place, groups, weights, scale, terms, dtype, name):
    rows = groups[0][0].shape[1] * len(groups)
    blocks = [block for group in groups for block in group]
    vmem = pl.BlockSpec(memory_space=pltpu.VMEM)
    return pl.pallas_call(
        functools.partial(
            output_kernel, groups=len(groups), count=len(weights)
        ),
        in_specs=[pl.BlockSpec(memory_space=pltpu.SMEM)]
        + [vmem] * len(blocks)
        + [pl.BlockSpec(memory_space=pl.ANY)] * len(weights)
        + [vmem] * (1 + len(terms)),
        out_specs=vmem,
        scratch_shapes=[
            pltpu.VMEM((16, 4, 32, WIDE), jnp.bfloat16),
            pltpu.SemaphoreType.DMA((4,)),
        ],
        out_shape=jax.ShapeDtypeStruct((rows, WIDE), dtype),
        compiler_params=pltpu.CompilerParams(vmem_limit_bytes=VMEM_LIMIT),
        cost_estimate=cost(2 * rows * 2048 * WIDE),
        name=name,
    )(place, *blocks, *weights, scale, *terms)


def body(hidden, modulation, qkv_weight, out_weight, control_proj, cached_mlp):
    hidden, cached = hidden[0], cached_mlp[0]
    mod = modulation[0]
    branch = lax.axis_index("branch")
    y = lax.axis_index("tp")
    s = lax.axis_index("seq")
    z = lax.rem(s // 2, 4)
    place = jnp.stack([y, z, branch, lax.rem(s, 2), s // 8]).astype(jnp.int32)
    gates = lax.dynamic_slice_in_dim(mod[2:4], y * WIDE, WIDE, 1)
    turn = lambda by: lax.rem(y + by, 4)
    rows = ROWS // 2
    weight = qkv_weight[0].transpose(1, 0, 2)

    def sent_y(value):
        cut = lambda by: lax.dynamic_slice_in_dim(value, turn(by) * WIDE, WIDE, 1)
        return [cut(0)] + [along_y(cut(by), by) for by in (1, 2, 3)]

    def heads_turned(part):
        return [part[0]] + [along_z(part[by], by) for by in (1, 2, 3)]

    tokens = lax.all_gather(hidden, "tp", axis=1, tiled=True)

    with jax.named_scope("out_weight_columns"):
        share = lax.dynamic_slice_in_dim(out_weight[0], s * 32, 32, 0)
        turned = jnp.stack(sent_y(share))
        ordered = jnp.stack(
            [lax.dynamic_index_in_dim(turned, turn(4 - row), 0, keepdims=False) for row in range(4)]
        )
        of_x = jnp.stack([ordered, across_x(ordered)])
        of_xz = [of_x] + [along_z(of_x, by) for by in (1, 2, 3)]

    base = (hidden.astype(jnp.float32) + gates[1] * cached.astype(jnp.float32)).astype(jnp.bfloat16)
    sent = lax.ppermute(base[rows:], "branch", [(0, 1)])
    base = after(jnp.where(branch == 0, base[:rows], sent), *of_xz)
    gated = (ordered.reshape(128, WIDE).astype(jnp.float32) * gates[0]).astype(jnp.bfloat16)
    joint, early = products(gated, base, control_proj)
    joint_share = lax.psum_scatter(joint, "tp", scatter_dimension=1, tiled=True)

    projected = qkv(place, tokens, mod, weight, [joint, early])
    with jax.named_scope("early_residual"):
        early = lax.psum_scatter(early, "tp", scatter_dimension=1, tiled=True)


    turned = heads_turned(projected)
    with jax.named_scope("out_weight_columns"):
        of_xz = jnp.stack(after(of_xz, projected)).reshape(8, 4, 32, WIDE)
        out_columns = [of_xz, across_cores(of_xz)]
    query = jnp.concatenate([block[0] for block in turned], axis=0)
    near = jnp.concatenate([block[1:3] for block in turned], axis=1)
    far = across_x(near)
    carry = attention(query, [near, across_cores(near)], [], False, 0, 1, out_columns)
    far = after(far, carry)
    with jax.named_scope("joint_weight"):
        joint_share = after(joint_share, near).reshape(4, 32, WIDE)
        joint_columns = lax.all_gather(joint_share, "seq", axis=0)
    attended = attention(query, [far, across_cores(far)], carry, True, 0, 1, [early])

    attended = attended.reshape(4, ROWS, HEAD_DIM)
    attended = [attended[0]] + [along_z(attended[by], 4 - by) for by in (1, 2, 3)]
    halves = []
    for half in range(2):
        part = jnp.stack([block[half * rows : (half + 1) * rows] for block in attended])
        halves.append([part, *gathered_y(part)])
    joined = []
    for half in range(2):
        terms = [early] if half == 0 else []
        residual = output(place, halves[half : half + 1], [joint_columns], gates, terms, jnp.bfloat16, "residual")
        joined.append(lax.ppermute(residual, "branch", [(0, 1)]))
    terms = [hidden, cached, early]
    blended = output(place, halves, out_columns, gates, terms, jnp.float32, "blended")
    joined = jnp.concatenate(joined, axis=0)
    return (blended + joined.astype(jnp.float32)).astype(jnp.bfloat16)[None]


def solution(mesh):
    placed = (
        P("branch", "seq", "tp"),
        P("branch", None, None),
        P("branch", None, None, "tp"),
        P("branch", "tp", None),
        P("tp", None),
        P("branch", "seq", "tp"),
    )
    return jax.shard_map(
        body, mesh=mesh, in_specs=placed, out_specs=P("branch", "seq", "tp"), check_vma=False
    )
```

```python
import functools

import jax
import jax.numpy as jnp
from jax import lax
from jax.experimental import pallas as pl
from jax.experimental.pallas import tpu as pltpu
from jax.sharding import PartitionSpec as P

HEAD_DIM = 128
ROWS = 512
WIDE = 1024
COLS = 512
HEADS_HERE = 4
Q_SCALE = 1.4426950408889634 / HEAD_DIM**0.5
NT = (((1,), (1,)), ((), ()))
VMEM_LIMIT = 58 * 2**20


def cost(flops):
    return pl.CostEstimate(flops=int(flops), bytes_accessed=2**20, transcendentals=0)


def seq_pairs(move):
    where = [(h, z, c) for h in range(2) for z in range(4) for c in range(2)]
    index = lambda h, z, c: h * 8 + z * 2 + c
    return [(index(*p), index(*move(*p))) for p in where]


def along_z(value, by):
    return lax.ppermute(value, "seq", seq_pairs(lambda h, z, c: (h, (z + by) % 4, c)))


def across_x(value):
    return lax.ppermute(value, "seq", seq_pairs(lambda h, z, c: (1 - h, z, c)))


def across_cores(value):
    return lax.ppermute(value, "seq", seq_pairs(lambda h, z, c: (h, z, 1 - c)))


def along_y(value, by):
    return lax.ppermute(value, "tp", [(i, (i + by) % 4) for i in range(4)])


def after(value, *others):
    return lax.optimization_barrier((value, others))[0]


def gathered_y(value):
    one, three = along_y(value, 1), along_y(value, 3)
    return [one, along_y(value, 2), three]


def qkv_kernel(place, tokens, mod, weight, *rest):
    out, modulated, held, arrived, whole, landed = rest[-6:]
    z = place[1]
    rows = modulated.shape[0]
    quarter = rows // 4
    tile = 16
    lands = []
    for part in range(4):
        here = pl.ds(part * quarter, quarter)
        lands.append(pltpu.make_async_copy(tokens.at[here], whole.at[here], landed.at[part]))
    copies = []
    for c in range(3):
        for k in range(4):
            here = pl.ds(k * WIDE, WIDE)
            copies.append(
                pltpu.make_async_copy(weight.at[c, here], held.at[c, here], arrived.at[c * 4 + k])
            )
    for copy in lands + copies[:4]:
        copy.start()

    for first in range(0, rows, tile):
        if first % quarter == 0:
            lands[first // quarter].wait()
            if first // quarter in (1, 2):
                for copy in copies[first // quarter * 4 : first // quarter * 4 + 4]:
                    copy.start()
        here = pl.ds(first, tile)
        total = 0.0
        for k in range(4):
            part = whole[here, k * WIDE : (k + 1) * WIDE].astype(jnp.float32)
            total = total + jnp.sum(part, axis=1, keepdims=True)
        mean = total * (1.0 / (4 * WIDE))
        square = 0.0
        for k in range(4):
            part = whole[here, k * WIDE : (k + 1) * WIDE].astype(jnp.float32) - mean
            square = square + jnp.sum(part * part, axis=1, keepdims=True)
        scale = lax.rsqrt(square * (1.0 / (4 * WIDE)) + 1e-06)
        for k in range(4):
            columns = pl.ds(k * WIDE, WIDE)
            part = (whole[here, columns].astype(jnp.float32) - mean) * scale
            value = part * (1.0 + mod[1:2, columns]) + mod[0:1, columns]
            modulated[here, columns] = value.astype(jnp.bfloat16)

    for c in range(3):
        for copy in copies[c * 4 : c * 4 + 4]:
            copy.wait()
        product = jnp.dot(modulated[...], held[c], preferred_element_type=jnp.float32)
        if c == 0:
            product = product * Q_SCALE
        product = product.astype(jnp.bfloat16)
        for head in range(HEADS_HERE):
            slot = lax.rem(head + 4 - z, 4)
            out[slot, c] = product[:, head * HEAD_DIM : (head + 1) * HEAD_DIM]


def qkv(place, tokens, mod, weight, earlier):
    rows = tokens.shape[0]
    hbm = pl.BlockSpec(memory_space=pl.ANY)
    vmem = pl.BlockSpec(memory_space=pltpu.VMEM)
    return pl.pallas_call(
        qkv_kernel,
        in_specs=[pl.BlockSpec(memory_space=pltpu.SMEM), hbm, vmem, hbm] + [hbm] * len(earlier),
        out_specs=vmem,
        scratch_shapes=[
            pltpu.VMEM((rows, 4 * WIDE), jnp.bfloat16),
            pltpu.VMEM((3, 4 * WIDE, COLS), jnp.bfloat16),
            pltpu.SemaphoreType.DMA((12,)),
            pltpu.VMEM((rows, 4 * WIDE), jnp.bfloat16),
            pltpu.SemaphoreType.DMA((4,)),
        ],
        out_shape=jax.ShapeDtypeStruct((4, 3, rows, HEAD_DIM), jnp.bfloat16),
        compiler_params=pltpu.CompilerParams(vmem_limit_bytes=VMEM_LIMIT),
        cost_estimate=cost(2 * rows * 4 * WIDE * 3 * COLS),
        name="qkv",
    )(place, tokens, mod, weight, *earlier)


def products_kernel(one, two, right, out_one, out_two):
    for left, out in ((one, out_one), (two, out_two)):
        out[...] = jnp.dot(left[...], right[...], preferred_element_type=jnp.float32).astype(out.dtype)


def products(one, two, right):
    depth, columns = right.shape
    rows = (one.shape[0], two.shape[0])
    return pl.pallas_call(
        products_kernel,
        grid=(columns // WIDE,),
        in_specs=[pl.BlockSpec((count, depth), lambda n: (0, 0)) for count in rows]
        + [pl.BlockSpec((depth, WIDE), lambda n: (0, n))],
        out_specs=[pl.BlockSpec((count, WIDE), lambda n: (0, n)) for count in rows],
        out_shape=[jax.ShapeDtypeStruct((count, columns), jnp.bfloat16) for count in rows],
        compiler_params=pltpu.CompilerParams(vmem_limit_bytes=VMEM_LIMIT),
        cost_estimate=cost(2 * sum(rows) * depth * columns),
        name="products",
    )(one, two, right)


def attention_kernel(*refs, count, gates, first, last):
    refs, held = refs[:-1], refs[-1]
    for index in range(4):

        @pl.when(pl.program_id(0) == index)
        def _(index=index):
            held[...] = refs[index][0]

    query = held[...]
    pairs = refs[4 : 4 + count]
    rest = refs[4 + count + gates :]
    rows = query.shape[0]
    pieces = []
    for pair in pairs:
        step = pair.shape[1] // pl.cdiv(pair.shape[1], 1024)
        pieces += [(pair, pl.ds(at, step)) for at in range(0, pair.shape[1], step)]

    def scores_of(piece):
        pair, at = piece
        keys = pair[0, at, :]
        return lax.dot_general(query, keys, NT, preferred_element_type=jnp.float32)

    if first:
        top = jnp.full((rows, 1), -1e30, jnp.float32)
        total = jnp.zeros((rows, 1), jnp.float32)
        weighted = jnp.zeros((rows, HEAD_DIM), jnp.float32)
    else:
        weighted = rest[0][...]
        top = jnp.max(rest[1][...], axis=1, keepdims=True)
        total = jnp.max(rest[2][...], axis=1, keepdims=True)
        rest = rest[3:]
    ready = scores_of(pieces[0])
    for index, (pair, at) in enumerate(pieces):
        scores = ready
        if index + 1 < len(pieces):
            ready = scores_of(pieces[index + 1])
        new_top = jnp.maximum(top, jnp.max(scores, axis=1, keepdims=True))
        weights = jnp.exp2(scores - new_top)
        fade = jnp.exp2(top - new_top)
        total = total * fade + jnp.sum(weights, axis=1, keepdims=True)
        values = pair[1, at, :]
        update = jnp.dot(weights.astype(jnp.bfloat16), values, preferred_element_type=jnp.float32)
        weighted = weighted * fade + update
        top = new_top
    if last:
        rest[0][...] = (weighted / total).astype(jnp.bfloat16)
    else:
        rest[0][...] = weighted
        rest[1][...] = jnp.broadcast_to(top, (rows, HEAD_DIM))
        rest[2][...] = jnp.broadcast_to(total, (rows, HEAD_DIM))


def attention(turned, pairs, carry, last, earlier=()):
    block = turned[0].shape[1]
    rows = 4 * block
    tokens = sum(pair.shape[1] for pair in pairs)
    row_block = pl.BlockSpec((block, HEAD_DIM), lambda i: (i, 0))
    shape = lambda dtype: jax.ShapeDtypeStruct((rows, HEAD_DIM), dtype)
    if last:
        out_shape, out_specs = shape(jnp.bfloat16), row_block
    else:
        out_shape, out_specs = [shape(jnp.float32)] * 3, [row_block] * 3
    return pl.pallas_call(
        functools.partial(attention_kernel, count=len(pairs), gates=len(earlier), first=not carry, last=last),
        grid=(rows // block,),
        in_specs=[pl.BlockSpec((1, block, HEAD_DIM), lambda i: (0, 0, 0))] * 4
        + [pl.BlockSpec(pair.shape, lambda i: (0, 0, 0)) for pair in pairs]
        + [pl.BlockSpec(memory_space=pl.ANY)] * len(earlier)
        + [row_block] * len(carry),
        out_specs=out_specs,
        scratch_shapes=[pltpu.VMEM((block, HEAD_DIM), jnp.bfloat16)],
        out_shape=out_shape,
        compiler_params=pltpu.CompilerParams(vmem_limit_bytes=VMEM_LIMIT),
        cost_estimate=pl.CostEstimate(
            flops=4 * rows * tokens * HEAD_DIM,
            bytes_accessed=4 * tokens * HEAD_DIM,
            transcendentals=rows * tokens,
        ),
        name="attention",
    )(*turned, *pairs, *earlier, *carry)


def output_kernel(place, *refs, groups, count):
    blocks, refs = refs[: 4 * groups], refs[4 * groups :]
    weights, scale, terms = refs[:count], refs[count], refs[count + 1 : -3]
    out, held, arrived = refs[-3:]
    y, z, branch, core, x_hi = place[0], place[1], place[2], place[3], place[4]
    rows = out.shape[0]
    copies = []
    for index in range(4):
        to = held.at[pl.ds(index * 4, 4)]
        per = 4 // count
        source = weights[index // per].at[pl.ds(index % per * 4, 4)]
        copies.append(pltpu.make_async_copy(source, to, arrived.at[index]))
        copies[-1].start()

    def rows_of(back, by):
        row, head = lax.rem(y + 4 - back, 4), lax.rem(z + by, 4)
        if count == 1:
            return held[pl.ds(head * 4, 4), row].reshape(HEAD_DIM, WIDE)
        parts = []
        for i in range(4):
            across = lax.rem(head // 2 + x_hi, 2)
            behind = lax.rem(z + 4 - lax.rem(head, 2) * 2 - i // 2, 4)
            parts.append(held[lax.rem(i % 2 + core, 2) * 8 + behind * 2 + across, row])
        return jnp.concatenate(parts, axis=0)

    for copy in copies:
        copy.wait()
    products = [None] * groups
    for back in range(4):
        share = jnp.concatenate([rows_of(back, by) for by in range(4)], axis=0)
        for group in range(groups):
            block = blocks[4 * group + back]
            left = jnp.concatenate([block[by] for by in range(4)], axis=1)
            update = jnp.dot(left, share, preferred_element_type=jnp.float32)
            products[group] = update if back == 0 else products[group] + update
    if count == 1:
        product = products[0]
        if terms:
            product = product + terms[0][...].astype(jnp.float32)
        out[...] = product.astype(out.dtype)
    else:
        for group in range(groups):
            here = pl.ds(group * (rows // groups), rows // groups)
            value = terms[0][here, :].astype(jnp.float32) + scale[0:1, :] * products[group]
            value = value + scale[1:2, :] * terms[1][here, :].astype(jnp.float32)
            if group == 1:
                value = value + branch.astype(jnp.float32) * terms[2][...].astype(jnp.float32)
            out[here, :] = value


def output(place, groups, weights, scale, terms, dtype, name):
    rows = groups[0][0].shape[1] * len(groups)
    blocks = [block for group in groups for block in group]
    vmem = pl.BlockSpec(memory_space=pltpu.VMEM)
    return pl.pallas_call(
        functools.partial(
            output_kernel, groups=len(groups), count=len(weights)
        ),
        in_specs=[pl.BlockSpec(memory_space=pltpu.SMEM)]
        + [vmem] * len(blocks)
        + [pl.BlockSpec(memory_space=pl.ANY)] * len(weights)
        + [vmem] * (1 + len(terms)),
        out_specs=vmem,
        scratch_shapes=[
            pltpu.VMEM((16, 4, 32, WIDE), jnp.bfloat16),
            pltpu.SemaphoreType.DMA((4,)),
        ],
        out_shape=jax.ShapeDtypeStruct((rows, WIDE), dtype),
        compiler_params=pltpu.CompilerParams(vmem_limit_bytes=VMEM_LIMIT),
        cost_estimate=cost(2 * rows * 2048 * WIDE),
        name=name,
    )(place, *blocks, *weights, scale, *terms)


def body(hidden, modulation, qkv_weight, out_weight, control_proj, cached_mlp):
    hidden, cached = hidden[0], cached_mlp[0]
    mod = modulation[0]
    branch = lax.axis_index("branch")
    y = lax.axis_index("tp")
    s = lax.axis_index("seq")
    z = lax.rem(s // 2, 4)
    place = jnp.stack([y, z, branch, lax.rem(s, 2), s // 8]).astype(jnp.int32)
    gates = lax.dynamic_slice_in_dim(mod[2:4], y * WIDE, WIDE, 1)
    turn = lambda by: lax.rem(y + by, 4)
    rows = ROWS // 2
    weight = qkv_weight[0].transpose(1, 0, 2)

    def sent_y(value):
        cut = lambda by: lax.dynamic_slice_in_dim(value, turn(by) * WIDE, WIDE, 1)
        return [cut(0)] + [along_y(cut(by), by) for by in (1, 2, 3)]

    def heads_turned(part):
        return [part[0]] + [along_z(part[by], by) for by in (1, 2, 3)]

    tokens = lax.all_gather(hidden, "tp", axis=1, tiled=True)

    with jax.named_scope("out_weight_columns"):
        share = lax.dynamic_slice_in_dim(out_weight[0], s * 32, 32, 0)
        turned = jnp.stack(sent_y(share))
        ordered = jnp.stack(
            [lax.dynamic_index_in_dim(turned, turn(4 - row), 0, keepdims=False) for row in range(4)]
        )
        of_x = jnp.stack([ordered, across_x(ordered)])
        of_xz = [of_x] + [along_z(of_x, by) for by in (1, 2, 3)]

    base = (hidden.astype(jnp.float32) + gates[1] * cached.astype(jnp.float32)).astype(jnp.bfloat16)
    sent = lax.ppermute(base[rows:], "branch", [(0, 1)])
    base = after(jnp.where(branch == 0, base[:rows], sent), *of_xz)
    gated = (ordered.reshape(128, WIDE).astype(jnp.float32) * gates[0]).astype(jnp.bfloat16)
    joint, early = products(gated, base, control_proj)
    joint_share = lax.psum_scatter(joint, "tp", scatter_dimension=1, tiled=True)

    projected = qkv(place, tokens, mod, weight, [joint, early])
    with jax.named_scope("early_residual"):
        early = lax.psum_scatter(early, "tp", scatter_dimension=1, tiled=True)


    turned = heads_turned(projected)
    with jax.named_scope("out_weight_columns"):
        of_xz = jnp.stack(after(of_xz, projected)).reshape(8, 4, 32, WIDE)
        out_columns = [of_xz, across_cores(of_xz)]
    near = jnp.concatenate([block[1:3] for block in turned], axis=1)
    far = across_x(near)
    carry = attention(turned, [near, across_cores(near)], [], False, out_columns)
    far = after(far, carry)
    with jax.named_scope("joint_weight"):
        joint_share = after(joint_share, near).reshape(4, 32, WIDE)
        joint_columns = lax.all_gather(joint_share, "seq", axis=0)
    attended = attention(turned, [far, across_cores(far)], carry, True, [early])

    attended = attended.reshape(4, ROWS, HEAD_DIM)
    attended = [attended[0]] + [along_z(attended[by], 4 - by) for by in (1, 2, 3)]
    halves = []
    for half in range(2):
        part = jnp.stack([block[half * rows : (half + 1) * rows] for block in attended])
        halves.append([part, *gathered_y(part)])
    joined = []
    for half in range(2):
        terms = [early] if half == 0 else []
        residual = output(place, halves[half : half + 1], [joint_columns], gates, terms, jnp.bfloat16, "residual")
        joined.append(lax.ppermute(residual, "branch", [(0, 1)]))
    terms = [hidden, cached, early]
    blended = output(place, halves, out_columns, gates, terms, jnp.float32, "blended")
    joined = jnp.concatenate(joined, axis=0)
    return (blended + joined.astype(jnp.float32)).astype(jnp.bfloat16)[None]


def solution(mesh):
    placed = (
        P("branch", "seq", "tp"),
        P("branch", None, None),
        P("branch", None, None, "tp"),
        P("branch", "tp", None),
        P("tp", None),
        P("branch", "seq", "tp"),
    )
    return jax.shard_map(
        body, mesh=mesh, in_specs=placed, out_specs=P("branch", "seq", "tp"), check_vma=False
    )
```
